32 devices in a mesh: groups: 2 (over y), adapter: 4 (over x, core), tensor: 4 (over z).
Axes of the slice: x: 2, y: 2, z: 4, core: 2. Of those that a mesh axis runs over, the one named last changes fastest.
Arguments:
- hidden: bfloat16 [1024, 28672], P(('groups', 'adapter'), 'tensor'), parts along dimension 0, may hold values from -6 to 6
- base_down_weight: bfloat16 [28672, 8192], P('tensor', 'adapter'), may hold values from -0.03125 to 0.03125
- adapter_input_factors: bfloat16 [32, 28672, 64], P('adapter', 'tensor'), may hold values from -0.03125 to 0.03125
- adapter_output_factors: bfloat16 [32, 64, 8192], P(None, 'tensor', 'adapter'), may hold values from -0.75 to 0.75
- adapter_of_request: int32 [1024, 1], P('groups'), parts along dimension 0, may hold values from 0 to 31; in each aligned block of 128 rows (0 to 127, 128 to 255, ...) at most 4 rows name the same one
Outputs:
- mixed: bfloat16 [1024, 8192], P(('groups', 'tensor'), 'adapter'), parts along dimension 0
The draws below stay inside these ranges and needn't reach their ends.
There are 2 independent parts, one for each index of `groups`. The reference program is written for one: setup_inputs(seed, part) draws one part's arguments, and reference() takes and returns one part's arrays. A program takes and returns all parts, laid end to end along the dimension named above; an argument that names none is the same for every part. Nothing has to cross between parts.
Inputs may be any that keep to these rules, and one draw needn't show every extreme that they name: `adapter_of_request`: in each aligned block of 128 rows no adapter is named by more than 4 rows, a bound that some block reaches.
All inputs are finite; a program needn't handle non-finite values.
Results may differ from the reference program's by a relative error of at most 0.0039.
Values may be sent and summed in bfloat16 or wider, within the bound.
A program may use at most 128 MiB of HBM per device.

```python
import math
import jax
import jax.numpy as jnp
import numpy as np
from jax import lax

MODEL_WIDTH = 8192
HIDDEN_UNITS = 28672
ADAPTER_RANK = 64
MOST = 4
ROWS_DEV = 128
ADAPTER_TOTAL = 32
ROWS = 512
N_ADAPTER = 4


def block_levels(key, extent, split, smallest, top_value):
    level = 1.0
    for dim, blocks in split:
        steps = jax.random.uniform(jax.random.fold_in(jax.random.fold_in(key, 6), dim), (blocks,), jnp.float32, smallest / len(split), top_value / len(split))
        level = level * jnp.repeat(jnp.exp(steps), extent[dim] // blocks).reshape((-1,) + (1,) * (len(extent) - 1 - dim))
    return level


def assign_block(rng, own, number, rows, number_of, top, reach, slope):
    sequence = jax.random.permutation(rng, number_of)
    crowded, usual = shares(number_of, rows * top, reach, slope, True), shares(number_of, rows * top, reach, slope, False)
    places = jnp.arange(number_of)

    def named(sizes, rotation):
        used = int((sizes > 0).sum())
        fixed = max(1, used // 4)
        moved = fixed + (places - fixed + rotation * (used - fixed)) % max(1, number_of - fixed)
        return jnp.zeros((number_of,), jnp.int32).at[sequence[jnp.where(places < fixed, places, moved)]].set(jnp.asarray(sizes, jnp.int32))

    sizes = jnp.where(number % 4 == 0, named(crowded, number // 4), named(usual, number - number // 4 - 1))
    mixed = jax.random.permutation(jax.random.fold_in(own, 3), number_of)
    donor, receiver = mixed[0:number_of // 2 * 2:2], mixed[1:number_of // 2 * 2:2]
    margin = jnp.minimum(sizes[donor] - 1, reach - sizes[receiver]) // 2
    margin = jnp.where((donor == sequence[0]) | (receiver == sequence[0]) | (sizes[receiver] == 0), 0, jnp.maximum(margin, 0))
    moved = jax.random.randint(jax.random.fold_in(own, 4), (number_of // 2,), 0, 1 << 20) % (margin + 1)
    sizes = sizes.at[donor].add(-moved).at[receiver].add(moved)
    members = jnp.searchsorted(jnp.cumsum(sizes), jnp.arange(rows * top), side="right").astype(jnp.int32)
    grid = members.reshape(top, rows).T
    grid = grid[jax.random.permutation(jax.random.fold_in(own, 1), rows)]
    rotation = jax.random.randint(jax.random.fold_in(own, 2), (rows, 1), 0, top)
    return jnp.take_along_axis(grid, (jnp.arange(top)[None, :] + rotation) % top, axis=1)


def shares(number_of, total, bound, skew, full):
    weights = [(1 << 20) // math.isqrt(grade ** skew) + 1 for grade in range(1, number_of + 1)]
    largest = bound if full else min(bound, max(-(-total // number_of), total * weights[0] // sum(weights)))
    least = 1 if total - largest >= number_of - 1 else 0
    given, rest = [largest] + [least] * (number_of - 1), total - largest - least * (number_of - 1)
    while rest > 0:
        candidates = [i for i in range(1, number_of) if given[i] < largest] or [i for i in range(1, number_of) if given[i] < bound]
        mass, remaining = sum([weights[i] for i in candidates]), rest
        for i in candidates:
            more = min(bound - given[i], max(1, remaining * weights[i] // mass), rest)
            given[i] = given[i] + more
            rest = rest - more
    return np.array(given)


def bell_draw(rng, extent, deviation, limit, cuts=(), kind=jnp.bfloat16):
    result = deviation * jax.random.normal(rng, extent, jnp.float32)
    if cuts:
        result = result * block_levels(rng, extent, cuts, -0.22, 0.18)
    return jnp.clip(result, -limit, limit).astype(kind)


def setup_inputs(seed: int = 0, part: int = 0) -> dict:
    key_of = jax.random.split(jax.random.key(seed), 6)
    own_keys = jax.random.split(jax.random.fold_in(key_of[5], part), 6)
    hidden = bell_draw(own_keys[0], (ROWS, HIDDEN_UNITS), 1.0, 6.0, ((0, 4), (1, 4)))
    base_down_weight = bell_draw(key_of[1], (HIDDEN_UNITS, MODEL_WIDTH), HIDDEN_UNITS ** -0.5, 0.03125, ((0, 4), (1, 4)))
    adapter_input_factors = bell_draw(key_of[2], (ADAPTER_TOTAL, HIDDEN_UNITS, ADAPTER_RANK), HIDDEN_UNITS ** -0.5, 0.03125, ((0, 4), (1, 4)))
    adapter_output_factors = bell_draw(key_of[3], (ADAPTER_TOTAL, ADAPTER_RANK, MODEL_WIDTH), ADAPTER_RANK ** -0.5, 0.75, ((1, 4), (2, 4)))
    adapter_of_request_keys = jax.random.split(jax.random.fold_in(own_keys[4], 1), ROWS // ROWS_DEV)
    adapter_of_request_turns = jax.random.permutation(jax.random.fold_in(own_keys[4], 3), ROWS // ROWS_DEV)
    adapter_of_request = jax.vmap(lambda own, number: assign_block(jax.random.fold_in(own_keys[4], 2), own, number, ROWS_DEV, ADAPTER_TOTAL, 1, MOST, 2))(adapter_of_request_keys, adapter_of_request_turns).reshape((ROWS, 1))
    return dict(hidden=hidden, base_down_weight=base_down_weight, adapter_input_factors=adapter_input_factors, adapter_output_factors=adapter_output_factors, adapter_of_request=adapter_of_request)


def slot_numbers(flat_ids, blocks, block_rows):
    grouped = flat_ids.reshape(blocks, block_rows)
    matches = grouped[:, :, None] == grouped[:, None, :]
    position = jnp.arange(block_rows, dtype=jnp.int32)
    earlier = position[None, :] < position[:, None]
    within = jnp.sum((matches & earlier[None]).astype(jnp.int32), axis=2).reshape(-1)
    sources = jnp.arange(blocks * block_rows, dtype=jnp.int32) // block_rows
    return flat_ids * (blocks * MOST) + sources * MOST + within


def reference(hidden, base_down_weight, adapter_input_factors, adapter_output_factors, adapter_of_request):
    flat_ids = adapter_of_request[:, 0].astype(jnp.int32)
    adapter_wise = N_ADAPTER * MOST
    slot_position = slot_numbers(flat_ids, N_ADAPTER, ROWS_DEV)
    slot_row_block = jnp.full((ADAPTER_TOTAL * adapter_wise,), -1, jnp.int32)
    slot_row_block = slot_row_block.at[slot_position].set(jnp.arange(ROWS, dtype=jnp.int32))
    slot_row_block = slot_row_block.reshape(ADAPTER_TOTAL, adapter_wise)

    def single_adapter(packed):
        rows_here, a_matrix, output_factor = packed
        selected_factor = hidden[jnp.clip(rows_here, 0, ROWS - 1)]
        selected_factor = jnp.where((rows_here >= 0)[:, None], selected_factor, jnp.zeros((), hidden.dtype))
        low = jnp.dot(selected_factor, a_matrix, preferred_element_type=jnp.float32).astype(jnp.bfloat16)
        return jnp.dot(low, output_factor, preferred_element_type=jnp.float32)

    adapter_slot_table = lax.map(single_adapter, (slot_row_block, adapter_input_factors, adapter_output_factors))
    adapter_delta = adapter_slot_table.reshape(ADAPTER_TOTAL * adapter_wise, MODEL_WIDTH)[slot_position]
    base_result = jnp.dot(hidden, base_down_weight, preferred_element_type=jnp.float32)
    return (base_result + adapter_delta).astype(jnp.bfloat16)
```

```python
import jax
import jax.numpy as jnp
from jax import lax
from jax.sharding import PartitionSpec as P


def shards(
    hidden, base_down_weight, adapter_input_factors, adapter_output_factors, adapter_of_request
):
    owner_index = lax.axis_index("adapter")
    adapters_resident = adapter_input_factors.shape[0]
    every_adapter = adapter_output_factors.shape[0]
    rank_segment = adapter_output_factors.shape[1]
    flat_ids = adapter_of_request[:, 0]
    total_rows = flat_ids.shape[0]
    gathered = lax.all_gather(hidden, "adapter", axis=0, tiled=True)
    dense = jnp.einsum(
        "rb,nbh->rnh", gathered, adapter_input_factors, preferred_element_type=jnp.float32
    )
    here = owner_index * adapters_resident + jnp.arange(adapters_resident, dtype=jnp.int32)
    owned = flat_ids[:, None] == here[None, :]
    low_part = jnp.sum(jnp.where(owned[:, :, None], dense, 0.0), axis=1)
    low_mine = lax.psum_scatter(
        low_part, "tensor", scatter_dimension=1, tiled=True
    ).astype(jnp.bfloat16)
    low_rows = lax.psum(low_mine, "adapter")
    one_hot = flat_ids[:, None] == jnp.arange(every_adapter, dtype=jnp.int32)[None, :]
    spread = jnp.where(one_hot[:, :, None], low_rows[:, None, :], jnp.zeros((), jnp.bfloat16))
    spread = spread.reshape(total_rows, every_adapter * rank_segment)
    output_factor = adapter_output_factors.reshape(
        every_adapter * rank_segment, adapter_output_factors.shape[2]
    )
    base_part = jnp.dot(gathered, base_down_weight, preferred_element_type=jnp.float32)
    part = base_part + jnp.dot(spread, output_factor, preferred_element_type=jnp.float32)
    return lax.psum_scatter(
        part.astype(jnp.bfloat16), "tensor", scatter_dimension=0, tiled=True
    )


def solution(mesh):
    return jax.shard_map(
        shards,
        mesh=mesh,
        in_specs=(
            P(("groups", "adapter"), "tensor"),
            P("tensor", "adapter"),
            P("adapter", "tensor", None),
            P(None, "tensor", "adapter"),
            P("groups", None),
        ),
        out_specs=P(("groups", "tensor"), "adapter"),
        check_vma=False,
    )
```

```python
import functools
import jax
import jax.numpy as jnp
from jax import lax
from jax.experimental import pallas as pl
from jax.experimental.pallas import tpu as pltpu
from jax.sharding import PartitionSpec as P

CHUNK = 32
TILE = 256
F32 = jnp.float32
BF16 = jnp.bfloat16


def kernel(
    na, nt, ids_ref, hidden, weight, in_t, out_f, out_ref,
    w_v, in_v, of_v, rows_v, acc, low_mine, low_recv, bc_mine, bc_recv, rs_mine, rs_recv,
    load_sem, x_ss, x_rs, core_ss, core_rs, fwd_ss, fwd_rs,
    low_ss, low_rs, bc_ss, bc_rs, rs_ss, rs_rs,
):
    rounds, _, chunk, depth = rows_v.shape
    chips = na // 2
    per = na // nt
    width = weight.shape[1]
    total = na * chunk
    residents = in_t.shape[0] // (nt * low_mine.shape[2])
    rank = nt * low_mine.shape[2]
    seg = low_mine.shape[2]
    every = out_f.shape[0] // seg
    me_a = lax.axis_index("adapter")
    me_t = lax.axis_index("tensor")
    core = lax.rem(me_a, 2)
    chip = me_a // 2
    partner = me_a + 1 - 2 * core

    def to_a(a):
        return {"adapter": a}

    def to_t(t):
        return {"tensor": t}

    def rdma(src, dst, ss, rs, dev):
        return pltpu.make_async_remote_copy(
            src_ref=src, dst_ref=dst, send_sem=ss, recv_sem=rs,
            device_id=dev, device_id_type=pl.DeviceIdType.MESH,
        )

    loads = [
        pltpu.make_async_copy(hidden, rows_v.at[:, me_a], load_sem.at[0]),
        pltpu.make_async_copy(in_t, in_v, load_sem.at[1]),
        pltpu.make_async_copy(weight, w_v, load_sem.at[2]),
        pltpu.make_async_copy(out_f, of_v, load_sem.at[3]),
    ]

    barrier = pltpu.get_barrier_semaphore()
    for d in range(1, na):
        pl.semaphore_signal(
            barrier, inc=1, device_id=to_a(lax.rem(me_a + d, na)),
            device_id_type=pl.DeviceIdType.MESH,
        )
    for d in range(1, nt):
        pl.semaphore_signal(
            barrier, inc=1, device_id=to_t(lax.rem(me_t + d, nt)),
            device_id_type=pl.DeviceIdType.MESH,
        )
    loads[0].start()
    loads[1].start()
    pl.semaphore_wait(barrier, na - 1 + nt - 1)

    def x_send(i, d):
        there = lax.rem(chip + d, chips) * 2 + core
        return rdma(
            hidden.at[i], rows_v.at[i, me_a], x_ss.at[i, d], x_rs.at[i, d], to_a(there)
        )

    def core_send(i):
        return rdma(
            hidden.at[i], rows_v.at[i, me_a], core_ss.at[i], core_rs.at[i], to_a(partner)
        )

    def fwd_send(i, d):
        block = lax.rem(chip + chips - d, chips) * 2 + core
        return rdma(
            rows_v.at[i, block], rows_v.at[i, block],
            fwd_ss.at[i, d], fwd_rs.at[i, d], to_a(partner),
        )

    def low_send(i, d):
        t = lax.rem(me_t + d, nt)
        return rdma(
            low_mine.at[i, t], low_recv.at[i, d], low_ss.at[i, d], low_rs.at[i, d], to_t(t)
        )

    def bc_send(i, d):
        a = lax.rem(me_a + d, na)
        return rdma(
            bc_mine.at[i], bc_recv.at[i, d], bc_ss.at[i, d], bc_rs.at[i, d], to_a(a)
        )

    def rs_send(i, d):
        t = lax.rem(me_t + d, nt)
        return rdma(
            rs_mine.at[i, t], rs_recv.at[i, d], rs_ss.at[i, d], rs_rs.at[i, d], to_t(t)
        )

    for i in range(min(2, rounds)):
        for d in range(1, chips):
            x_send(i, d).start()
        core_send(i).start()
    loads[2].start()
    loads[3].start()
    for i in range(2, rounds):
        core_send(i).start()

    def front(i):
        for d in range(1, chips):
            x_send(i, d).wait_recv()
            fwd_send(i, d).start()
        for d in range(1, chips):
            x_send(i, d).wait_send()

        @pl.when(i + 2 < rounds)
        def _():
            for d in range(1, chips):
                x_send(i + 2, d).start()

    def middle(i, first):
        core_send(i).wait_recv()
        for d in range(1, chips):
            fwd_send(i, d).wait_recv()
        if first:
            loads[0].wait()
            loads[1].wait()
        ids = ids_ref[i]
        low = jnp.zeros((rank, total), F32)
        here = rows_v[i].reshape(total, depth)
        projected = lax.dot_general(
            in_v[...], here, (((1,), (1,)), ((), ())), preferred_element_type=F32
        )
        for n in range(residents):
            low = low + jnp.where(
                ids == me_a * residents + n, projected[n * rank:(n + 1) * rank], 0.0
            )
        low_mine[i] = low.reshape(nt, seg, total)
        for d in range(1, nt):
            low_send(i, d).start()
        if first:
            loads[2].wait()
            loads[3].wait()

        def tile(j, carry):
            cols = pl.ds(pl.multiple_of(j * TILE, TILE), TILE)
            part = jnp.dot(
                rows_v[i].reshape(total, depth), w_v[:, cols], preferred_element_type=F32
            )
            acc[i, :, :, cols] = part.reshape(nt, per * chunk, TILE)
            return carry

        lax.fori_loop(0, width // TILE, tile, 0)
        summed = low_mine[i, me_t]
        for d in range(1, nt):
            low_send(i, d).wait_recv()
            summed = summed + low_recv[i, d]
        bc_mine[i] = summed.astype(BF16).astype(F32)
        for d in range(1, na):
            bc_send(i, d).start()

    def back(i):
        rows_low = bc_mine[i]
        for d in range(1, na):
            bc_send(i, d).wait_recv()
            rows_low = rows_low + bc_recv[i, d]
        ids = ids_ref[i]
        which = lax.broadcasted_iota(jnp.int32, (every, 1, total), 0)
        spread = jnp.where(which == ids[None], rows_low[None], 0.0)
        spread = spread.reshape(every * seg, total).T.astype(BF16)

        def tile(j, carry):
            cols = pl.ds(pl.multiple_of(j * TILE, TILE), TILE)
            part = jnp.dot(spread, of_v[:, cols], preferred_element_type=F32)
            part = acc[i, :, :, cols] + part.reshape(nt, per * chunk, TILE)
            acc[i, :, :, cols] = part
            rs_mine[i, :, :, cols] = part.astype(BF16)
            return carry

        lax.fori_loop(0, width // TILE, tile, 0)
        for d in range(1, nt):
            rs_send(i, d).start()

    front(0)
    middle(0, True)

    def body(i, carry):
        front(i)
        back(i - 1)
        middle(i, False)
        return carry

    lax.fori_loop(1, rounds, body, 0)
    back(rounds - 1)

    def finish(i, carry):
        val = acc[i, me_t]
        for d in range(1, nt):
            rs_send(i, d).wait_recv()
            val = val + rs_recv[i, d].astype(F32)
        out_ref[:, i] = val.reshape(per, chunk, width).astype(BF16)
        for d in range(1, chips):
            fwd_send(i, d).wait_send()
        core_send(i).wait_send()
        for d in range(1, nt):
            low_send(i, d).wait_send()
            rs_send(i, d).wait_send()
        for d in range(1, na):
            bc_send(i, d).wait_send()
        return carry

    lax.fori_loop(0, rounds, finish, 0)


def shards(na, nt, hidden, weight, in_f, out_f, ids):
    rows_local, depth = hidden.shape
    width = weight.shape[1]
    residents, _, rank = in_f.shape
    every, seg, _ = out_f.shape
    chunk = CHUNK
    rounds = rows_local // chunk
    per = na // nt
    chips = na // 2
    total = na * chunk
    in_t = jnp.transpose(in_f, (0, 2, 1)).reshape(residents * rank, depth)
    out_f = out_f.reshape(every * seg, width)
    ids = ids.reshape(na, rounds, chunk).transpose(1, 0, 2).reshape(rounds, 1, total)
    hidden = hidden.reshape(rounds, chunk, depth)
    dma = pltpu.SemaphoreType.DMA
    anywhere = pl.BlockSpec(memory_space=pl.ANY)
    vmem = pl.BlockSpec(memory_space=pltpu.VMEM)
    flops = 2 * na * rows_local * depth * (width + residents * rank)
    out = pl.pallas_call(
        functools.partial(kernel, na, nt),
        out_shape=jax.ShapeDtypeStruct((per, rounds, chunk, width), BF16),
        in_specs=[vmem, anywhere, anywhere, anywhere, anywhere],
        out_specs=vmem,
        scratch_shapes=[
            pltpu.VMEM((depth, width), BF16),
            pltpu.VMEM((residents * rank, depth), BF16),
            pltpu.VMEM((every * seg, width), BF16),
            pltpu.VMEM((rounds, na, chunk, depth), BF16),
            pltpu.VMEM((rounds, nt, per * chunk, width), F32),
            pltpu.VMEM((rounds, nt, seg, total), F32),
            pltpu.VMEM((rounds, nt, seg, total), F32),
            pltpu.VMEM((rounds, seg, total), F32),
            pltpu.VMEM((rounds, na, seg, total), F32),
            pltpu.VMEM((rounds, nt, per * chunk, width), BF16),
            pltpu.VMEM((rounds, nt, per * chunk, width), BF16),
            dma((4,)),
            dma((rounds, chips)), dma((rounds, chips)),
            dma((rounds,)), dma((rounds,)),
            dma((rounds, chips)), dma((rounds, chips)),
            dma((rounds, nt)), dma((rounds, nt)),
            dma((rounds, na)), dma((rounds, na)),
            dma((rounds, nt)), dma((rounds, nt)),
        ],
        compiler_params=pltpu.CompilerParams(
            collective_id=0, has_side_effects=True, vmem_limit_bytes=63 * 1024 * 1024
        ),
        cost_estimate=pl.CostEstimate(
            flops=flops, bytes_accessed=2 * depth * width, transcendentals=0
        ),
    )(ids, hidden, weight, in_t, out_f)
    return out.reshape(per * rows_local, width)


def solution(mesh):
    return jax.shard_map(
        functools.partial(shards, mesh.shape["adapter"], mesh.shape["tensor"]),
        mesh=mesh,
        in_specs=(
            P(("groups", "adapter"), "tensor"),
            P("tensor", "adapter"),
            P("adapter", "tensor", None),
            P(None, "tensor", "adapter"),
            P("groups", None),
        ),
        out_specs=P(("groups", "tensor"), "adapter"),
        check_vma=False,
    )
```

```python
import functools
import jax
import jax.numpy as jnp
from jax import lax
from jax.experimental import pallas as pl
from jax.experimental.pallas import tpu as pltpu
from jax.sharding import PartitionSpec as P

CHUNK = 32
TILE = 256
F32 = jnp.float32
BF16 = jnp.bfloat16


def kernel(
    na, nt, ids_ref, hidden, weight, in_t, out_f, out_ref,
    w_v, in_v, of_v, rows_v, acc, low_mine, low_recv, bc_mine, bc_recv, rs_mine, rs_recv,
    load_sem, x_ss, x_rs, core_ss, core_rs, fwd_ss, fwd_rs,
    low_ss, low_rs, bc_ss, bc_rs, rs_ss, rs_rs, *hop,
):
    rounds, _, chunk, depth = rows_v.shape
    chips = na // 2
    per = na // nt
    width = weight.shape[1]
    total = na * chunk
    residents = in_t.shape[0] // (nt * low_mine.shape[2])
    rank = nt * low_mine.shape[2]
    seg = low_mine.shape[2]
    every = out_f.shape[0] // seg
    me_a = lax.axis_index("adapter")
    me_t = lax.axis_index("tensor")
    core = lax.rem(me_a, 2)
    chip = me_a // 2
    partner = me_a + 1 - 2 * core
    two_hop = nt == 4
    if two_hop:
        hop_recv, hop_ss, hop_rs = hop
        near = me_t + 1 - 2 * lax.rem(me_t, 2)
        far = 2 - 2 * (me_t // 2)
        outer = lax.rem(me_t, nt - 1) == 0
        inner = lax.rem(me_t, nt - 1) != 0

    def to_a(a):
        return {"adapter": a}

    def to_t(t):
        return {"tensor": t}

    def rdma(src, dst, ss, rs, dev):
        return pltpu.make_async_remote_copy(
            src_ref=src, dst_ref=dst, send_sem=ss, recv_sem=rs,
            device_id=dev, device_id_type=pl.DeviceIdType.MESH,
        )

    loads = [
        pltpu.make_async_copy(hidden, rows_v.at[:, me_a], load_sem.at[0]),
        pltpu.make_async_copy(in_t, in_v, load_sem.at[1]),
        pltpu.make_async_copy(weight, w_v, load_sem.at[2]),
        pltpu.make_async_copy(out_f, of_v, load_sem.at[3]),
    ]

    barrier = pltpu.get_barrier_semaphore()
    for d in range(1, na):
        pl.semaphore_signal(
            barrier, inc=1, device_id=to_a(lax.rem(me_a + d, na)),
            device_id_type=pl.DeviceIdType.MESH,
        )
    for d in range(1, nt):
        pl.semaphore_signal(
            barrier, inc=1, device_id=to_t(lax.rem(me_t + d, nt)),
            device_id_type=pl.DeviceIdType.MESH,
        )
    loads[0].start()
    loads[1].start()
    pl.semaphore_wait(barrier, na - 1 + nt - 1)

    def x_send(i, d):
        there = lax.rem(chip + d, chips) * 2 + core
        return rdma(
            hidden.at[i], rows_v.at[i, me_a], x_ss.at[i, d], x_rs.at[i, d], to_a(there)
        )

    def core_send(i):
        return rdma(
            hidden.at[i], rows_v.at[i, me_a], core_ss.at[i], core_rs.at[i], to_a(partner)
        )

    def fwd_send(i, d):
        block = lax.rem(chip + chips - d, chips) * 2 + core
        return rdma(
            rows_v.at[i, block], rows_v.at[i, block],
            fwd_ss.at[i, d], fwd_rs.at[i, d], to_a(partner),
        )

    def low_send(i, d):
        t = lax.rem(me_t + d, nt)
        return rdma(
            low_mine.at[i, t], low_recv.at[i, d], low_ss.at[i, d], low_rs.at[i, d], to_t(t)
        )

    def bc_send(i, d):
        a = lax.rem(me_a + d, na)
        return rdma(
            bc_mine.at[i], bc_recv.at[i, d], bc_ss.at[i, d], bc_rs.at[i, d], to_a(a)
        )

    def rs_send(i, d):
        t = lax.rem(me_t + d, nt)
        return rdma(
            rs_mine.at[i, t], rs_recv.at[i, d], rs_ss.at[i, d], rs_rs.at[i, d], to_t(t)
        )

    def near_send(i):
        return rdma(
            rs_mine.at[i, near], rs_recv.at[i, 1], rs_ss.at[i, 1], rs_rs.at[i, 1], to_t(near)
        )

    def hop_send(i, k):
        return rdma(
            rs_mine.at[i, far + k], hop_recv.at[i, k], hop_ss.at[i, k], hop_rs.at[i, k],
            to_t(near),
        )

    def far_send(i, k):
        return rdma(
            rs_mine.at[i, far + k], rs_recv.at[i, 2], rs_ss.at[i, 2 + k], rs_rs.at[i, 2],
            to_t(far + k),
        )

    for d in range(1, chips):
        x_send(0, d).start()
    core_send(0).start()
    loads[2].start()
    loads[3].start()

    def front(i):
        for d in range(1, chips):
            x_send(i, d).wait_recv()
            fwd_send(i, d).start()
        for d in range(1, chips):
            x_send(i, d).wait_send()

        @pl.when(i + 1 < rounds)
        def _():
            for d in range(1, chips):
                x_send(i + 1, d).start()
            core_send(i + 1).start()

    def middle(i, first):
        core_send(i).wait_recv()
        for d in range(1, chips):
            fwd_send(i, d).wait_recv()
        if first:
            loads[0].wait()
            loads[1].wait()
        ids = ids_ref[i]
        low = jnp.zeros((rank, total), F32)
        here = rows_v[i].reshape(total, depth)
        projected = lax.dot_general(
            in_v[...], here, (((1,), (1,)), ((), ())), preferred_element_type=F32
        )
        for n in range(residents):
            low = low + jnp.where(
                ids == me_a * residents + n, projected[n * rank:(n + 1) * rank], 0.0
            )
        low_mine[i] = low.reshape(nt, seg, total)
        for d in range(1, nt):
            low_send(i, d).start()
        if first:
            loads[2].wait()
            loads[3].wait()

        def tile(j, carry):
            cols = pl.ds(pl.multiple_of(j * TILE, TILE), TILE)
            part = jnp.dot(
                rows_v[i].reshape(total, depth), w_v[:, cols], preferred_element_type=F32
            )
            acc[i, :, :, cols] = part.reshape(nt, per * chunk, TILE)
            return carry

        lax.fori_loop(0, width // TILE, tile, 0)
        summed = low_mine[i, me_t]
        for d in range(1, nt):
            low_send(i, d).wait_recv()
            summed = summed + low_recv[i, d]
        bc_mine[i] = summed.astype(BF16).astype(F32)
        for d in range(1, na):
            bc_send(i, d).start()

    def back(i):
        rows_low = bc_mine[i]
        for d in range(1, na):
            bc_send(i, d).wait_recv()
            rows_low = rows_low + bc_recv[i, d]
        ids = ids_ref[i]
        which = lax.broadcasted_iota(jnp.int32, (every, 1, total), 0)
        spread = jnp.where(which == ids[None], rows_low[None], 0.0)
        spread = spread.reshape(every * seg, total).T.astype(BF16)

        def tile(j, carry):
            cols = pl.ds(pl.multiple_of(j * TILE, TILE), TILE)
            part = jnp.dot(spread, of_v[:, cols], preferred_element_type=F32)
            part = acc[i, :, :, cols] + part.reshape(nt, per * chunk, TILE)
            acc[i, :, :, cols] = part
            rs_mine[i, :, :, cols] = part.astype(BF16)
            return carry

        lax.fori_loop(0, width // TILE, tile, 0)
        if not two_hop:
            for d in range(1, nt):
                rs_send(i, d).start()
            return

        @pl.when(outer)
        def _():
            for k in range(2):
                hop_send(i, k).start()

        near_send(i).start()

    def relay(i):
        if not two_hop:
            return

        @pl.when(inner)
        def _():
            for k in range(1, -1, -1):
                hop_send(i, k).wait_recv()
                joined = acc[i, far + k] + hop_recv[i, k].astype(F32)
                rs_mine[i, far + k] = joined.astype(BF16)
                far_send(i, k).start()

    front(0)
    middle(0, True)
    back(0)

    def body(i, carry):
        front(i)
        middle(i, False)
        relay(i - 1)
        back(i)
        return carry

    lax.fori_loop(1, rounds, body, 0)
    relay(rounds - 1)

    def finish(i, carry):
        val = acc[i, me_t]
        if two_hop:
            near_send(i).wait_recv()
            far_send(i, 0).wait_recv()
            val = val + (rs_recv[i, 1].astype(F32) + rs_recv[i, 2].astype(F32))
        else:
            for d in range(1, nt):
                rs_send(i, d).wait_recv()
                val = val + rs_recv[i, d].astype(F32)
        out_ref[:, i] = val.reshape(per, chunk, width).astype(BF16)
        for d in range(1, chips):
            fwd_send(i, d).wait_send()
        core_send(i).wait_send()
        for d in range(1, nt):
            low_send(i, d).wait_send()
            if not two_hop:
                rs_send(i, d).wait_send()
        if two_hop:
            near_send(i).wait_send()

            @pl.when(outer)
            def _():
                for k in range(2):
                    hop_send(i, k).wait_send()

            @pl.when(inner)
            def _():
                for k in range(2):
                    far_send(i, k).wait_send()
        for d in range(1, na):
            bc_send(i, d).wait_send()
        return carry

    lax.fori_loop(0, rounds, finish, 0)


def shards(na, nt, hidden, weight, in_f, out_f, ids):
    rows_local, depth = hidden.shape
    width = weight.shape[1]
    residents, _, rank = in_f.shape
    every, seg, _ = out_f.shape
    chunk = CHUNK
    rounds = rows_local // chunk
    per = na // nt
    chips = na // 2
    total = na * chunk
    in_t = jnp.transpose(in_f, (0, 2, 1)).reshape(residents * rank, depth)
    out_f = out_f.reshape(every * seg, width)
    ids = ids.reshape(na, rounds, chunk).transpose(1, 0, 2).reshape(rounds, 1, total)
    hidden = hidden.reshape(rounds, chunk, depth)
    dma = pltpu.SemaphoreType.DMA
    hop = []
    if nt == 4:
        hop = [
            pltpu.VMEM((rounds, 2, per * chunk, width), BF16),
            dma((rounds, 2)), dma((rounds, 2)),
        ]
    anywhere = pl.BlockSpec(memory_space=pl.ANY)
    vmem = pl.BlockSpec(memory_space=pltpu.VMEM)
    flops = 2 * na * rows_local * depth * (width + residents * rank)
    out = pl.pallas_call(
        functools.partial(kernel, na, nt),
        out_shape=jax.ShapeDtypeStruct((per, rounds, chunk, width), BF16),
        in_specs=[vmem, anywhere, anywhere, anywhere, anywhere],
        out_specs=vmem,
        scratch_shapes=[
            pltpu.VMEM((depth, width), BF16),
            pltpu.VMEM((residents * rank, depth), BF16),
            pltpu.VMEM((every * seg, width), BF16),
            pltpu.VMEM((rounds, na, chunk, depth), BF16),
            pltpu.VMEM((rounds, nt, per * chunk, width), F32),
            pltpu.VMEM((rounds, nt, seg, total), F32),
            pltpu.VMEM((rounds, nt, seg, total), F32),
            pltpu.VMEM((rounds, seg, total), F32),
            pltpu.VMEM((rounds, na, seg, total), F32),
            pltpu.VMEM((rounds, nt, per * chunk, width), BF16),
            pltpu.VMEM((rounds, nt, per * chunk, width), BF16),
            dma((4,)),
            dma((rounds, chips)), dma((rounds, chips)),
            dma((rounds,)), dma((rounds,)),
            dma((rounds, chips)), dma((rounds, chips)),
            dma((rounds, nt)), dma((rounds, nt)),
            dma((rounds, na)), dma((rounds, na)),
            dma((rounds, nt)), dma((rounds, nt)),
        ] + hop,
        compiler_params=pltpu.CompilerParams(
            collective_id=0, has_side_effects=True, vmem_limit_bytes=63 * 1024 * 1024
        ),
        cost_estimate=pl.CostEstimate(
            flops=flops, bytes_accessed=2 * depth * width, transcendentals=0
        ),
    )(ids, hidden, weight, in_t, out_f)
    return out.reshape(per * rows_local, width)


def solution(mesh):
    return jax.shard_map(
        functools.partial(shards, mesh.shape["adapter"], mesh.shape["tensor"]),
        mesh=mesh,
        in_specs=(
            P(("groups", "adapter"), "tensor"),
            P("tensor", "adapter"),
            P("adapter", "tensor", None),
            P(None, "tensor", "adapter"),
            P("groups", None),
        ),
        out_specs=P(("groups", "tensor"), "adapter"),
        check_vma=False,
    )
```

```python
import functools
import jax
import jax.numpy as jnp
from jax import lax
from jax.experimental import pallas as pl
from jax.experimental.pallas import tpu as pltpu
from jax.sharding import PartitionSpec as P

CHUNK = 32
TILE = 256
F32 = jnp.float32
BF16 = jnp.bfloat16


def kernel(
    na, nt, ids_ref, hidden, weight, in_t, out_f, out_ref,
    w_v, in_v, of_v, rows_v, acc, low_mine, low_recv, bc_mine, bc_recv, rs_mine, rs_recv,
    load_sem, x_ss, x_rs, core_ss, core_rs, fwd_ss, fwd_rs,
    low_ss, low_rs, bc_ss, bc_rs, rs_ss, rs_rs, ids_v, *hop,
):
    rounds, _, chunk, depth = rows_v.shape
    chips = na // 2
    per = na // nt
    width = weight.shape[1]
    total = na * chunk
    residents = in_t.shape[0] // (nt * low_mine.shape[2])
    rank = nt * low_mine.shape[2]
    seg = low_mine.shape[2]
    every = out_f.shape[0] // seg
    me_a = lax.axis_index("adapter")
    me_t = lax.axis_index("tensor")
    core = lax.rem(me_a, 2)
    chip = me_a // 2
    partner = me_a + 1 - 2 * core
    two_hop = nt == 4
    if two_hop:
        hop_recv, hop_ss, hop_rs = hop
        near = me_t + 1 - 2 * lax.rem(me_t, 2)
        far = 2 - 2 * (me_t // 2)
        outer = lax.rem(me_t, nt - 1) == 0
        inner = lax.rem(me_t, nt - 1) != 0

    def to_a(a):
        return {"adapter": a}

    def to_t(t):
        return {"tensor": t}

    def rdma(src, dst, ss, rs, dev):
        return pltpu.make_async_remote_copy(
            src_ref=src, dst_ref=dst, send_sem=ss, recv_sem=rs,
            device_id=dev, device_id_type=pl.DeviceIdType.MESH,
        )

    loads = [
        pltpu.make_async_copy(hidden, rows_v.at[:, me_a], load_sem.at[0]),
        pltpu.make_async_copy(in_t, in_v, load_sem.at[1]),
        pltpu.make_async_copy(weight, w_v, load_sem.at[2]),
        pltpu.make_async_copy(out_f, of_v, load_sem.at[3]),
    ]

    barrier = pltpu.get_barrier_semaphore()
    for d in range(1, na):
        pl.semaphore_signal(
            barrier, inc=1, device_id=to_a(lax.rem(me_a + d, na)),
            device_id_type=pl.DeviceIdType.MESH,
        )
    for d in range(1, nt):
        pl.semaphore_signal(
            barrier, inc=1, device_id=to_t(lax.rem(me_t + d, nt)),
            device_id_type=pl.DeviceIdType.MESH,
        )
    for load in loads:
        load.start()
    pl.semaphore_wait(barrier, na - 1 + nt - 1)

    def x_send(i, d):
        there = lax.rem(chip + d, chips) * 2 + core
        return rdma(
            hidden.at[i], rows_v.at[i, me_a], x_ss.at[i, d], x_rs.at[i, d], to_a(there)
        )

    def core_send(i):
        return rdma(
            hidden.at[i], rows_v.at[i, me_a], core_ss.at[i], core_rs.at[i], to_a(partner)
        )

    def fwd_send(i, d):
        block = lax.rem(chip + chips - d, chips) * 2 + core
        return rdma(
            rows_v.at[i, block], rows_v.at[i, block],
            fwd_ss.at[i, d], fwd_rs.at[i, d], to_a(partner),
        )

    def low_send(i, d):
        t = lax.rem(me_t + d, nt)
        return rdma(
            low_mine.at[i, t], low_recv.at[i, d], low_ss.at[i, d], low_rs.at[i, d], to_t(t)
        )

    def bc_send(i, d):
        a = lax.rem(me_a + d, na)
        return rdma(
            bc_mine.at[i], bc_recv.at[i, d], bc_ss.at[i, d], bc_rs.at[i, d], to_a(a)
        )

    def rs_send(i, d):
        t = lax.rem(me_t + d, nt)
        return rdma(
            rs_mine.at[i, t], rs_recv.at[i, d], rs_ss.at[i, d], rs_rs.at[i, d], to_t(t)
        )

    def near_send(i):
        return rdma(
            rs_mine.at[i, near], rs_recv.at[i, 1], rs_ss.at[i, 1], rs_rs.at[i, 1], to_t(near)
        )

    def hop_send(i, k):
        return rdma(
            rs_mine.at[i, far + k], hop_recv.at[i, k], hop_ss.at[i, k], hop_rs.at[i, k],
            to_t(near),
        )

    def far_send(i, k):
        return rdma(
            rs_mine.at[i, far + k], rs_recv.at[i, 2], rs_ss.at[i, 2 + k], rs_rs.at[i, 2],
            to_t(far + k),
        )

    for d in range(1, chips):
        x_send(0, d).start()
    core_send(0).start()

    def front(i):
        for d in range(1, chips):
            x_send(i, d).wait_recv()
            fwd_send(i, d).start()
        for d in range(1, chips):
            x_send(i, d).wait_send()

        @pl.when(i + 1 < rounds)
        def _():
            for d in range(1, chips):
                x_send(i + 1, d).start()
            core_send(i + 1).start()

    def middle(i, first):
        core_send(i).wait_recv()
        for d in range(1, chips):
            fwd_send(i, d).wait_recv()
        if first:
            loads[0].wait()
            loads[1].wait()
        ids = ids_v[i]
        low = jnp.zeros((rank, total), F32)
        here = rows_v[i].reshape(total, depth)
        projected = lax.dot_general(
            in_v[...], here, (((1,), (1,)), ((), ())), preferred_element_type=F32
        )
        for n in range(residents):
            low = low + jnp.where(
                ids == me_a * residents + n, projected[n * rank:(n + 1) * rank], 0.0
            )
        low_mine[i] = low.reshape(nt, seg, total)
        for d in range(1, nt):
            low_send(i, d).start()
        if first:
            loads[2].wait()
            loads[3].wait()

        def tile(j, carry):
            cols = pl.ds(pl.multiple_of(j * TILE, TILE), TILE)
            part = jnp.dot(
                rows_v[i].reshape(total, depth), w_v[:, cols], preferred_element_type=F32
            )
            acc[i, :, :, cols] = part.reshape(nt, per * chunk, TILE)
            return carry

        tiles = width // TILE
        lax.fori_loop(0, tiles - tiles // 2, tile, 0)
        summed = low_mine[i, me_t]
        for d in range(1, nt):
            low_send(i, d).wait_recv()
            summed = summed + low_recv[i, d]
        bc_mine[i] = summed.astype(BF16).astype(F32)
        for d in range(1, na):
            bc_send(i, d).start()
        lax.fori_loop(tiles - tiles // 2, tiles, tile, 0)

    def back(i):
        rows_low = bc_mine[i]
        for d in range(1, na):
            bc_send(i, d).wait_recv()
            rows_low = rows_low + bc_recv[i, d]
        ids = ids_v[i]
        which = lax.broadcasted_iota(jnp.int32, (every, 1, total), 0)
        spread = jnp.where(which == ids[None], rows_low[None], 0.0)
        spread = spread.reshape(every * seg, total).T.astype(BF16)

        def tile(j, carry):
            cols = pl.ds(pl.multiple_of(j * TILE, TILE), TILE)
            part = jnp.dot(spread, of_v[:, cols], preferred_element_type=F32)
            part = acc[i, :, :, cols] + part.reshape(nt, per * chunk, TILE)
            acc[i, :, :, cols] = part
            rs_mine[i, :, :, cols] = part.astype(BF16)
            return carry

        lax.fori_loop(0, width // TILE, tile, 0)
        if not two_hop:
            for d in range(1, nt):
                rs_send(i, d).start()
            return

        @pl.when(outer)
        def _():
            for k in range(1, -1, -1):
                hop_send(i, k).start()

        near_send(i).start()

    def relay(i):
        if not two_hop:
            return

        @pl.when(inner)
        def _():
            for k in range(1, -1, -1):
                hop_send(i, k).wait_recv()
                joined = acc[i, far + k] + hop_recv[i, k].astype(F32)
                rs_mine[i, far + k] = joined.astype(BF16)
                far_send(i, k).start()

    for i in range(rounds):
        ids_v[i] = jnp.concatenate(
            [
                ids_ref[:, (a * rounds + i) * chunk:(a * rounds + i + 1) * chunk]
                for a in range(na)
            ],
            axis=1,
        )
    front(0)
    middle(0, True)
    if rounds > 1:
        front(1)
    back(0)

    def body(i, carry):
        middle(i, False)

        @pl.when(i + 1 < rounds)
        def _():
            front(i + 1)

        relay(i - 1)
        back(i)
        return carry

    lax.fori_loop(1, rounds, body, 0)

    def finish(i, carry):
        val = acc[i, me_t]
        if two_hop:
            near_send(i).wait_recv()
            far_send(i, 0).wait_recv()
            val = val + (rs_recv[i, 1].astype(F32) + rs_recv[i, 2].astype(F32))
        else:
            for d in range(1, nt):
                rs_send(i, d).wait_recv()
                val = val + rs_recv[i, d].astype(F32)
        out_ref[:, i] = val.reshape(per, chunk, width).astype(BF16)
        for d in range(1, chips):
            fwd_send(i, d).wait_send()
        core_send(i).wait_send()
        for d in range(1, nt):
            low_send(i, d).wait_send()
            if not two_hop:
                rs_send(i, d).wait_send()
        if two_hop:
            near_send(i).wait_send()

            @pl.when(outer)
            def _():
                for k in range(2):
                    hop_send(i, k).wait_send()

            @pl.when(inner)
            def _():
                for k in range(2):
                    far_send(i, k).wait_send()
        for d in range(1, na):
            bc_send(i, d).wait_send()
        return carry

    lax.fori_loop(0, rounds - 1, finish, 0)
    relay(rounds - 1)
    finish(rounds - 1, 0)


def shards(na, nt, hidden, weight, in_f, out_f, ids):
    rows_local, depth = hidden.shape
    width = weight.shape[1]
    residents, _, rank = in_f.shape
    every, seg, _ = out_f.shape
    chunk = CHUNK
    rounds = rows_local // chunk
    per = na // nt
    chips = na // 2
    total = na * chunk
    in_t = jnp.transpose(in_f, (0, 2, 1)).reshape(residents * rank, depth)
    out_f = out_f.reshape(every * seg, width)
    ids = ids.reshape(1, na * rows_local)
    hidden = hidden.reshape(rounds, chunk, depth)
    dma = pltpu.SemaphoreType.DMA
    hop = []
    if nt == 4:
        hop = [
            pltpu.VMEM((rounds, 2, per * chunk, width), BF16),
            dma((rounds, 2)), dma((rounds, 2)),
        ]
    anywhere = pl.BlockSpec(memory_space=pl.ANY)
    vmem = pl.BlockSpec(memory_space=pltpu.VMEM)
    flops = 2 * na * rows_local * depth * (width + residents * rank)
    out = pl.pallas_call(
        functools.partial(kernel, na, nt),
        out_shape=jax.ShapeDtypeStruct((per, rounds, chunk, width), BF16),
        in_specs=[vmem, anywhere, anywhere, anywhere, anywhere],
        out_specs=vmem,
        scratch_shapes=[
            pltpu.VMEM((depth, width), BF16),
            pltpu.VMEM((residents * rank, depth), BF16),
            pltpu.VMEM((every * seg, width), BF16),
            pltpu.VMEM((rounds, na, chunk, depth), BF16),
            pltpu.VMEM((rounds, nt, per * chunk, width), F32),
            pltpu.VMEM((rounds, nt, seg, total), F32),
            pltpu.VMEM((rounds, nt, seg, total), F32),
            pltpu.VMEM((rounds, seg, total), F32),
            pltpu.VMEM((rounds, na, seg, total), F32),
            pltpu.VMEM((rounds, nt, per * chunk, width), BF16),
            pltpu.VMEM((rounds, nt, per * chunk, width), BF16),
            dma((4,)),
            dma((rounds, chips)), dma((rounds, chips)),
            dma((rounds,)), dma((rounds,)),
            dma((rounds, chips)), dma((rounds, chips)),
            dma((rounds, nt)), dma((rounds, nt)),
            dma((rounds, na)), dma((rounds, na)),
            dma((rounds, nt)), dma((rounds, nt)),
            pltpu.VMEM((rounds, 1, total), jnp.int32),
        ] + hop,
        compiler_params=pltpu.CompilerParams(
            collective_id=0, has_side_effects=True, vmem_limit_bytes=63 * 1024 * 1024
        ),
        cost_estimate=pl.CostEstimate(
            flops=flops, bytes_accessed=2 * depth * width, transcendentals=0
        ),
    )(ids, hidden, weight, in_t, out_f)
    return out.reshape(per * rows_local, width)


def solution(mesh):
    return jax.shard_map(
        functools.partial(shards, mesh.shape["adapter"], mesh.shape["tensor"]),
        mesh=mesh,
        in_specs=(
            P(("groups", "adapter"), "tensor"),
            P("tensor", "adapter"),
            P("adapter", "tensor", None),
            P(None, "tensor", "adapter"),
            P("groups", None),
        ),
        out_specs=P(("groups", "tensor"), "adapter"),
        check_vma=False,
    )
```
